256 devices in a mesh: row: 16 (over x, z_hi), col: 16 (over y, z_lo, core).
Axes of the slice: x: 4, y: 4, z: 8 (z_hi: 4, z_lo: 2; z = z_hi * 2 + z_lo), core: 2. Of those that a mesh axis runs over, the one named last changes fastest.
Arguments:
- screened: float32 [12288, 12288], P('row', 'col'), may hold values from -0.0546875 to 0.0546875
- fit_coeffs: float32 [16, 12288, 256], P(None, 'row', 'col'), may hold values from -0.0546875 to 0.0546875
- coulomb_factors: float32 [16, 12288, 256], P(None, 'col', 'row'), may hold values from -6 to 6
- orbital_weights: float32 [16], replicated, may hold values from 0.2 to 2
Outputs:
- sigma: float32 [256, 256], P('row', 'col')
The draws below stay inside these ranges and needn't reach their ends.
All inputs are finite; a program needn't handle non-finite values.
Results may differ from the reference program's by a relative error of at most 0.00024.
Values sent between devices are 32-bit elements; how exact they have to be, the bound alone decides.
A program may use at most 128 MiB of HBM per device.

```python
import math
import jax
import jax.numpy as jnp
from jax import lax

NAUX = 12288
NS = 256
M = 16


def block_scale(key, dims, cuts, low, top_value):
    gain, own = 1.0, jax.random.fold_in(key, 6)
    for axis_at, blocks in cuts:
        heights = jnp.exp(jax.random.uniform(jax.random.fold_in(own, axis_at), (blocks,), jnp.float32, low / len(cuts), top_value / len(cuts)))
        gain = gain * jnp.repeat(heights, dims[axis_at] // blocks).reshape([-1 if axis == axis_at else 1 for axis in range(len(dims))])
    return gain


def bell_draw(key, shape, spread, most, split=(), held_as=jnp.bfloat16):
    drawn = jax.random.normal(key, shape, jnp.float32) * spread
    if len(split) > 0:
        drawn = block_scale(key, shape, split, -0.22, 0.18) * drawn
    return jnp.clip(drawn, min=-most, max=most).astype(held_as)


def setup_inputs(seed: int = 0) -> dict:
    arg_keys = jax.random.split(jax.random.key(seed), 5)
    screened = bell_draw(arg_keys[0], (NAUX, NAUX), NAUX ** -0.5, 0.0546875, ((0, 16), (1, 16)), jnp.float32)
    fit_coeffs = bell_draw(arg_keys[1], (M, NAUX, NS), NAUX ** -0.5, 0.0546875, ((1, 16), (2, 16)), jnp.float32)
    coulomb_factors = bell_draw(arg_keys[2], (M, NAUX, NS), 1.0, 6.0, ((1, 16), (2, 16)), jnp.float32)
    orbital_weights = jnp.clip(jnp.exp(jax.random.uniform(arg_keys[3], (M,), jnp.float32, math.log(0.2), math.log(2.0))), 0.2, 2.0)
    return {"screened": screened, "fit_coeffs": fit_coeffs, "coulomb_factors": coulomb_factors, "orbital_weights": orbital_weights}


def reference(screened, fit_coeffs, coulomb_factors, orbital_weights):
    def one_orbital(total, items):
        coef, factor, weight = items
        applied = jnp.dot(screened, factor, precision=lax.Precision.HIGHEST, preferred_element_type=jnp.float32)
        term = jnp.dot(coef.T, applied, precision=lax.Precision.HIGHEST, preferred_element_type=jnp.float32)
        return total + weight * term, None

    start_total = jnp.zeros((NS, NS), jnp.float32)
    sigma, unused = lax.scan(one_orbital, start_total, (fit_coeffs, coulomb_factors, orbital_weights))
    return sigma
```

```python
import functools

import jax
import jax.numpy as jnp
from jax import lax
from jax.experimental import pallas as pl
from jax.experimental.pallas import tpu as pltpu
from jax.sharding import PartitionSpec as P

MESH = pl.DeviceIdType.MESH
AHEAD = 2
LAG = 3
NT = (((1,), (1,)), ((), ()))


def split(v):
    high = v.astype(jnp.bfloat16)
    return high, (v - high.astype(jnp.float32)).astype(jnp.bfloat16)


def kernel(
    w_ref, c_ref, b_ref, scale_ref, out_ref,
    cbuf, bbuf, wfull, whigh, wlow, sig, part1, half, part2, turned,
    load_sem, c_recv, b_recv, c_send, b_send, recv1, recv2, send1, send2,
):
    orbitals, states, aux = c_ref.shape
    row, col = lax.axis_index("row"), lax.axis_index("col")
    x, zh = row // 4, row % 4
    y, zl, core = col // 4, (col // 2) % 2, col % 2

    def row_of(x_at, zh_at):
        return (x_at + 4) % 4 * 4 + (zh_at + 4) % 4

    def col_of(y_at, zl_at, core_at):
        return (y_at + 4) % 4 * 4 + zl_at * 2 + core_at

    barrier = pltpu.get_barrier_semaphore()
    for step in range(1, 16):
        pl.semaphore_signal(barrier, inc=1, device_id=(row, (col + step) % 16), device_id_type=MESH)
        pl.semaphore_signal(barrier, inc=1, device_id=((row + step) % 16, col), device_id_type=MESH)

    loads = [
        pltpu.make_async_copy(w_ref, wfull, load_sem.at[0]),
        pltpu.make_async_copy(c_ref, cbuf.at[col], load_sem.at[1]),
        pltpu.make_async_copy(b_ref, bbuf.at[row], load_sem.at[2]),
    ]
    for load in loads:
        load.start()
    sig[...] = jnp.zeros_like(sig)
    pl.semaphore_wait(barrier, 30)

    def c_copy(g, piece, edge, to, own=False):
        return pltpu.make_async_remote_copy(
            src_ref=c_ref.at[g] if own else cbuf.at[piece, g],
            dst_ref=cbuf.at[piece, g],
            send_sem=c_send.at[edge],
            recv_sem=c_recv.at[piece, g],
            device_id=(row, to),
            device_id_type=MESH,
        )

    def b_copy(g, piece, edge, to, own=False):
        return pltpu.make_async_remote_copy(
            src_ref=b_ref.at[g] if own else bbuf.at[piece, g],
            dst_ref=bbuf.at[piece, g],
            send_sem=b_send.at[edge],
            recv_sem=b_recv.at[piece, g],
            device_id=(to, col),
            device_id_type=MESH,
        )

    def own_sends(g):
        b_copy(g, row, 0, row_of(x, zh + 1), True).start()
        b_copy(g, row, 1, row_of(x, zh - 1), True).start()
        b_copy(g, row, 2, row_of(x + 1, zh), True).start()
        b_copy(g, row, 3, row_of(x - 1, zh), True).start()
        c_copy(g, col, 0, col_of(y, 1 - zl, core), True).start()
        c_copy(g, col, 1, col_of(y + 1, zl, core), True).start()
        c_copy(g, col, 2, col_of(y - 1, zl, core), True).start()
        c_copy(g, col, 3, col_of(y, zl, 1 - core), True).start()

    def got_c(g, piece):
        c_copy(g, piece, 0, col).wait_recv()

    def got_b(g, piece):
        b_copy(g, piece, 0, row).wait_recv()

    def first_hop(g):
        way = 1 - 2 * (g % 2)
        for at, side in enumerate((way, -way)):
            piece = row_of(x, zh - side)
            got_b(g, piece)
            if at == 0:
                b_copy(g, piece, 4, row_of(x, zh + way)).start()
            b_copy(g, piece, 5 + 2 * at, row_of(x + 1, zh)).start()
            b_copy(g, piece, 6 + 2 * at, row_of(x - 1, zh)).start()
        piece = col_of(y, 1 - zl, core)
        got_c(g, piece)
        c_copy(g, piece, 4, col_of(y + 1, zl, core)).start()
        c_copy(g, piece, 5, col_of(y - 1, zl, core)).start()
        c_copy(g, piece, 6, col_of(y, zl, 1 - core)).start()

    def second_hop(g):
        way = 1 - 2 * (g % 2)
        piece = row_of(x, zh + 2)
        got_b(g, piece)
        b_copy(g, piece, 9, row_of(x + 1, zh)).start()
        b_copy(g, piece, 10, row_of(x - 1, zh)).start()
        for at, off in enumerate((0, 1, -1, 2)):
            piece = row_of(x - way, zh + off)
            got_b(g, piece)
            b_copy(g, piece, 11 + at, row_of(x + way, zh)).start()
        for at in range(2):
            piece = col_of(y - way, at, core)
            got_c(g, piece)
            c_copy(g, piece, 7 + at, col_of(y + way, zl, core)).start()
            c_copy(g, piece, 9 + at, col_of(y, zl, 1 - core)).start()
            piece = col_of(y + way, at, core)
            got_c(g, piece)
            c_copy(g, piece, 11 + at, col_of(y, zl, 1 - core)).start()

    def third_hop(g):
        for at in range(2):
            piece = col_of(y + 2, at, core)
            got_c(g, piece)
            c_copy(g, piece, 13 + at, col_of(y, zl, 1 - core)).start()

    def products(g):
        way = 1 - 2 * (g % 2)
        for y_at in range(4):
            for zl_at in range(2):
                got_c(g, col_of(y_at, zl_at, 1 - core))
        c_high, c_low = split(cbuf[:, g].reshape(16 * states, aux))
        t = jnp.dot(c_high, whigh[...], preferred_element_type=jnp.float32)
        t += jnp.dot(c_high, wlow[...], preferred_element_type=jnp.float32)
        t += jnp.dot(c_low, whigh[...], preferred_element_type=jnp.float32)
        t_high, t_low = split(t * scale_ref[g])
        for off in range(4):
            got_b(g, row_of(x + way, zh + off))
            got_b(g, row_of(x + 2, zh + off))
        b_high, b_low = split(bbuf[:, g].reshape(16 * states, aux))
        s = lax.dot_general(b_high, t_high, NT, preferred_element_type=jnp.float32)
        s += lax.dot_general(b_high, t_low, NT, preferred_element_type=jnp.float32)
        s += lax.dot_general(b_low, t_high, NT, preferred_element_type=jnp.float32)
        sig[...] += s

    for g in range(AHEAD):
        own_sends(g)
    for load in loads:
        load.wait()
    w_high, w_low = split(wfull[...])
    whigh[...] = w_high
    wlow[...] = w_low

    @pl.loop(0, orbitals + LAG)
    def tick(t):
        @pl.when(t + AHEAD < orbitals)
        def _():
            own_sends(t + AHEAD)

        @pl.when(t < orbitals)
        def _():
            first_hop(t)

        @pl.when((t >= 1) & (t < orbitals + 1))
        def _():
            second_hop(t - 1)

        @pl.when((t >= 2) & (t < orbitals + 2))
        def _():
            third_hop(t - 2)

        @pl.when(t >= LAG)
        def _():
            products(t - LAG)

    def copy1(step):
        to = (col + step) % 16
        return pltpu.make_async_remote_copy(
            src_ref=sig.at[pl.ds(pl.multiple_of(to * states, states), states)],
            dst_ref=part1.at[col],
            send_sem=send1.at[step],
            recv_sem=recv1.at[col],
            device_id=(row, to),
            device_id_type=MESH,
        )

    def copy2(step):
        to = (row + step) % 16
        return pltpu.make_async_remote_copy(
            src_ref=half.at[to // 8],
            dst_ref=part2.at[row],
            send_sem=send2.at[step],
            recv_sem=recv2.at[row],
            device_id=(to, col),
            device_id_type=MESH,
        )

    for step in range(1, 16):
        copy1(step).start()
    total = sig[pl.ds(pl.multiple_of(col * states, states), states), :]
    for step in range(1, 16):
        piece = (col + step) % 16
        pltpu.make_async_copy(part1.at[piece], part1.at[piece], recv1.at[piece]).wait()
        total += part1[piece]
    half[0] = total[:, :128]
    half[1] = total[:, 128:]
    for step in range(1, 16):
        copy2(step).start()
    total = half[row // 8]
    for step in range(1, 16):
        piece = (row + step) % 16
        pltpu.make_async_copy(part2.at[piece], part2.at[piece], recv2.at[piece]).wait()
        total += part2[piece]
    turned[...] = total.T
    out_ref[...] = turned[pl.ds(pl.multiple_of(row % 8 * states, states), states), :]

    for step in range(1, 16):
        copy1(step).wait_send()
        copy2(step).wait_send()
    for edge in range(15):
        pltpu.make_async_copy(c_ref, cbuf.at[0], c_send.at[edge]).wait()
        pltpu.make_async_copy(b_ref, bbuf.at[0], b_send.at[edge]).wait()


def body(screened, fit_coeffs, coulomb_factors, orbital_weights):
    orbitals, aux, states = fit_coeffs.shape
    f32, bf16 = jnp.float32, jnp.bfloat16
    dma = pltpu.SemaphoreType.DMA
    return pl.pallas_call(
        kernel,
        out_shape=jax.ShapeDtypeStruct((states, states), f32),
        in_specs=[pl.BlockSpec(memory_space=pl.ANY)] * 3 + [pl.BlockSpec(memory_space=pltpu.SMEM)],
        out_specs=pl.BlockSpec(memory_space=pltpu.VMEM),
        scratch_shapes=[
            pltpu.VMEM((16, orbitals, states, aux), f32),
            pltpu.VMEM((16, orbitals, states, aux), f32),
            pltpu.VMEM((aux, aux), f32),
            pltpu.VMEM((aux, aux), bf16),
            pltpu.VMEM((aux, aux), bf16),
            pltpu.VMEM((16 * states, 16 * states), f32),
            pltpu.VMEM((16, states, 16 * states), f32),
            pltpu.VMEM((2, states, 128), f32),
            pltpu.VMEM((16, states, 128), f32),
            pltpu.VMEM((128, states), f32),
            dma((3,)),
            dma((16, orbitals)),
            dma((16, orbitals)),
            dma((15,)),
            dma((15,)),
            dma((16,)),
            dma((16,)),
            dma((16,)),
            dma((16,)),
        ],
        compiler_params=pltpu.CompilerParams(
            collective_id=0, has_side_effects=True, vmem_limit_bytes=48 * 1024 * 1024
        ),
        cost_estimate=pl.CostEstimate(flops=20_000_000_000, bytes_accessed=4_000_000, transcendentals=0),
    )(
        screened,
        jnp.transpose(fit_coeffs, (0, 2, 1)),
        jnp.transpose(coulomb_factors, (0, 2, 1)),
        orbital_weights,
    )


def solution(mesh):
    placed = (P("row", "col"), P(None, "row", "col"), P(None, "col", "row"), P())
    return jax.shard_map(
        body, mesh=mesh, in_specs=placed, out_specs=P("row", "col"), check_vma=False
    )
```

```python
import functools

import jax
import jax.numpy as jnp
from jax import lax
from jax.experimental import pallas as pl
from jax.experimental.pallas import tpu as pltpu
from jax.sharding import PartitionSpec as P

MESH = pl.DeviceIdType.MESH
AHEAD = 3
LAG = 4
X_FIRST = (4, 11)
B_RELAY, B_NEAR, B_FAR, B_SPREAD, B_LAST, B_KINDS = 0, 1, 2, 3, 6, 7
C_PAIR, C_NEAR, C_FAR, C_CORE, C_KINDS = 0, 1, 3, 5, 6
NT = (((1,), (1,)), ((), ()))


def split(v):
    high = v.astype(jnp.bfloat16)
    return high, (v - high.astype(jnp.float32)).astype(jnp.bfloat16)


def kernel(
    w_ref, c_ref, b_ref, scale_ref, out_ref,
    cbuf, bbuf, wfull, whigh, wlow, sig, part1, half, part2, turned,
    load_sem, c_recv, b_recv, c_send, b_send, recv1, recv2, send1, send2,
):
    orbitals, states, aux = c_ref.shape
    row, col = lax.axis_index("row"), lax.axis_index("col")
    x, zh = row // 4, row % 4
    y, zl, core = col // 4, (col // 2) % 2, col % 2

    def row_of(x_at, zh_at):
        return (x_at + 4) % 4 * 4 + (zh_at + 4) % 4

    def col_of(y_at, zl_at, core_at):
        return (y_at + 4) % 4 * 4 + zl_at * 2 + core_at

    barrier = pltpu.get_barrier_semaphore()
    for step in range(1, 16):
        pl.semaphore_signal(barrier, inc=1, device_id=(row, (col + step) % 16), device_id_type=MESH)
        pl.semaphore_signal(barrier, inc=1, device_id=((row + step) % 16, col), device_id_type=MESH)

    loads = [
        pltpu.make_async_copy(w_ref, wfull, load_sem.at[0]),
        pltpu.make_async_copy(c_ref, cbuf.at[col], load_sem.at[1]),
        pltpu.make_async_copy(b_ref, bbuf.at[row], load_sem.at[2]),
    ]
    for load in loads:
        load.start()
    sig[...] = jnp.zeros_like(sig)
    pl.semaphore_wait(barrier, 30)

    def c_copy(g, piece, edge, kind, to, own=False):
        return pltpu.make_async_remote_copy(
            src_ref=c_ref.at[g] if own else cbuf.at[piece, g],
            dst_ref=cbuf.at[piece, g],
            send_sem=c_send.at[edge],
            recv_sem=c_recv.at[kind, g],
            device_id=(row, to),
            device_id_type=MESH,
        )

    def b_copy(g, piece, edge, kind, to, own=False):
        return pltpu.make_async_remote_copy(
            src_ref=b_ref.at[g] if own else bbuf.at[piece, g],
            dst_ref=bbuf.at[piece, g],
            send_sem=b_send.at[edge],
            recv_sem=b_recv.at[kind, g],
            device_id=(to, col),
            device_id_type=MESH,
        )

    def got_c(g, kind, pieces=1):
        block = cbuf.at[pl.ds(0, pieces), g]
        pltpu.make_async_copy(block, block, c_recv.at[kind, g]).wait()

    def got_b(g, kind, pieces=1):
        block = bbuf.at[pl.ds(0, pieces), g]
        pltpu.make_async_copy(block, block, b_recv.at[kind, g]).wait()

    def route(g):
        x_first = jnp.where(functools.reduce(jnp.logical_or, [g == one for one in X_FIRST]), 1, 0)
        way = 1 - 2 * (g % 2)

        def at(first, second):
            return row_of(
                x + second + (first - second) * x_first, zh + first + (second - first) * x_first
            )

        return at, way

    def own_sends(g):
        at, way = route(g)
        b_copy(g, row, 0, B_RELAY, at(way, 0), True).start()
        b_copy(g, row, 1, B_NEAR, at(-way, 0), True).start()
        c_copy(g, col, 0, C_PAIR, col_of(y, 1 - zl, core), True).start()
        b_copy(g, row, 2, B_SPREAD, at(0, way), True).start()
        b_copy(g, row, 3, B_LAST, at(0, -way), True).start()
        c_copy(g, col, 1, C_NEAR, col_of(y + 1, zl, core), True).start()
        c_copy(g, col, 2, C_NEAR, col_of(y - 1, zl, core), True).start()
        c_copy(g, col, 3, C_CORE, col_of(y, zl, 1 - core), True).start()

    def first_hop(g):
        at, way = route(g)
        got_b(g, B_RELAY)
        piece = at(-way, 0)
        b_copy(g, piece, 4, B_FAR, at(way, 0)).start()
        b_copy(g, piece, 5, B_SPREAD + 1, at(0, way)).start()
        b_copy(g, piece, 6, B_LAST, at(0, -way)).start()
        got_b(g, B_NEAR)
        piece = at(way, 0)
        b_copy(g, piece, 7, B_SPREAD + 1, at(0, way)).start()
        b_copy(g, piece, 8, B_LAST, at(0, -way)).start()
        got_c(g, C_PAIR)
        piece = col_of(y, 1 - zl, core)
        c_copy(g, piece, 4, C_NEAR + 1, col_of(y + 1, zl, core)).start()
        c_copy(g, piece, 5, C_NEAR + 1, col_of(y - 1, zl, core)).start()
        c_copy(g, piece, 6, C_CORE, col_of(y, zl, 1 - core)).start()
        got_b(g, B_SPREAD)
        b_copy(g, at(0, -way), 9, B_LAST, at(0, way)).start()
        c_spread(g, 0, way)

    def c_spread(g, far, way):
        got_c(g, C_NEAR + far, 2)
        zl_at = zl + far - 2 * zl * far
        piece = col_of(y - way, zl_at, core)
        c_copy(g, piece, 7 + far, C_FAR + far, col_of(y + way, zl, core)).start()
        c_copy(g, piece, 9 + far, C_CORE, col_of(y, zl, 1 - core)).start()
        piece = col_of(y + way, zl_at, core)
        c_copy(g, piece, 11 + far, C_CORE, col_of(y, zl, 1 - core)).start()

    def c_far(g, far):
        got_c(g, C_FAR + far)
        piece = col_of(y + 2, zl + far - 2 * zl * far, core)
        c_copy(g, piece, 13 + far, C_CORE, col_of(y, zl, 1 - core)).start()

    def second_hop(g):
        at, way = route(g)
        got_b(g, B_FAR)
        piece = at(2, 0)
        b_copy(g, piece, 10, B_SPREAD + 2, at(0, way)).start()
        b_copy(g, piece, 11, B_LAST, at(0, -way)).start()
        got_b(g, B_SPREAD + 1, 2)
        b_copy(g, at(1, -way), 12, B_LAST, at(0, way)).start()
        b_copy(g, at(-1, -way), 13, B_LAST, at(0, way)).start()
        c_spread(g, 1, way)
        c_far(g, 0)

    def third_hop(g):
        at, way = route(g)
        got_b(g, B_SPREAD + 2)
        b_copy(g, at(2, -way), 14, B_LAST, at(0, way)).start()
        c_far(g, 1)

    def products(g):
        got_c(g, C_CORE, 8)
        c_high, c_low = split(cbuf[:, g].reshape(16 * states, aux))
        t = jnp.dot(c_high, whigh[...], preferred_element_type=jnp.float32)
        t += jnp.dot(c_high, wlow[...], preferred_element_type=jnp.float32)
        t += jnp.dot(c_low, whigh[...], preferred_element_type=jnp.float32)
        t_high, t_low = split(t * scale_ref[g])
        got_b(g, B_LAST, 8)
        b_high, b_low = split(bbuf[:, g].reshape(16 * states, aux))
        s = lax.dot_general(b_high, t_high, NT, preferred_element_type=jnp.float32)
        s += lax.dot_general(b_high, t_low, NT, preferred_element_type=jnp.float32)
        s += lax.dot_general(b_low, t_high, NT, preferred_element_type=jnp.float32)
        sig[...] += s

    for g in range(AHEAD):
        own_sends(g)
    for load in loads:
        load.wait()
    w_high, w_low = split(wfull[...])
    whigh[...] = w_high
    wlow[...] = w_low

    @pl.loop(0, orbitals + LAG)
    def tick(t):
        @pl.when(t + AHEAD < orbitals)
        def _():
            own_sends(t + AHEAD)

        @pl.when(t < orbitals)
        def _():
            first_hop(t)

        @pl.when((t >= 1) & (t < orbitals + 1))
        def _():
            second_hop(t - 1)

        @pl.when((t >= 2) & (t < orbitals + 2))
        def _():
            third_hop(t - 2)

        @pl.when(t >= LAG)
        def _():
            products(t - LAG)

    def copy1(step):
        to = (col + step) % 16
        return pltpu.make_async_remote_copy(
            src_ref=sig.at[pl.ds(pl.multiple_of(to * states, states), states)],
            dst_ref=part1.at[col],
            send_sem=send1.at[step],
            recv_sem=recv1.at[col],
            device_id=(row, to),
            device_id_type=MESH,
        )

    def copy2(step):
        to = (row + step) % 16
        return pltpu.make_async_remote_copy(
            src_ref=half.at[to // 8],
            dst_ref=part2.at[row],
            send_sem=send2.at[step],
            recv_sem=recv2.at[row],
            device_id=(to, col),
            device_id_type=MESH,
        )

    for step in range(1, 16):
        copy1(step).start()
    total = sig[pl.ds(pl.multiple_of(col * states, states), states), :]
    for step in range(1, 16):
        piece = (col + step) % 16
        pltpu.make_async_copy(part1.at[piece], part1.at[piece], recv1.at[piece]).wait()
        total += part1[piece]
    half[0] = total[:, :128]
    half[1] = total[:, 128:]
    for step in range(1, 16):
        copy2(step).start()
    total = half[row // 8]
    for step in range(1, 16):
        piece = (row + step) % 16
        pltpu.make_async_copy(part2.at[piece], part2.at[piece], recv2.at[piece]).wait()
        total += part2[piece]
    turned[...] = total.T
    out_ref[...] = turned[pl.ds(pl.multiple_of(row % 8 * states, states), states), :]

    for step in range(1, 16):
        copy1(step).wait_send()
        copy2(step).wait_send()
    for edge in range(15):
        pltpu.make_async_copy(c_ref, cbuf.at[0], c_send.at[edge]).wait()
        pltpu.make_async_copy(b_ref, bbuf.at[0], b_send.at[edge]).wait()


def body(screened, fit_coeffs, coulomb_factors, orbital_weights):
    orbitals, aux, states = fit_coeffs.shape
    f32, bf16 = jnp.float32, jnp.bfloat16
    dma = pltpu.SemaphoreType.DMA
    return pl.pallas_call(
        kernel,
        out_shape=jax.ShapeDtypeStruct((states, states), f32),
        in_specs=[pl.BlockSpec(memory_space=pl.ANY)] * 3 + [pl.BlockSpec(memory_space=pltpu.SMEM)],
        out_specs=pl.BlockSpec(memory_space=pltpu.VMEM),
        scratch_shapes=[
            pltpu.VMEM((16, orbitals, states, aux), f32),
            pltpu.VMEM((16, orbitals, states, aux), f32),
            pltpu.VMEM((aux, aux), f32),
            pltpu.VMEM((aux, aux), bf16),
            pltpu.VMEM((aux, aux), bf16),
            pltpu.VMEM((16 * states, 16 * states), f32),
            pltpu.VMEM((16, states, 16 * states), f32),
            pltpu.VMEM((2, states, 128), f32),
            pltpu.VMEM((16, states, 128), f32),
            pltpu.VMEM((128, states), f32),
            dma((3,)),
            dma((C_KINDS, orbitals)),
            dma((B_KINDS, orbitals)),
            dma((15,)),
            dma((15,)),
            dma((16,)),
            dma((16,)),
            dma((16,)),
            dma((16,)),
        ],
        compiler_params=pltpu.CompilerParams(
            collective_id=0, has_side_effects=True, vmem_limit_bytes=63 * 1024 * 1024
        ),
        cost_estimate=pl.CostEstimate(flops=20_000_000_000, bytes_accessed=4_000_000, transcendentals=0),
    )(
        screened,
        jnp.transpose(fit_coeffs, (0, 2, 1)),
        jnp.transpose(coulomb_factors, (0, 2, 1)),
        orbital_weights,
    )


def solution(mesh):
    placed = (P("row", "col"), P(None, "row", "col"), P(None, "col", "row"), P())
    return jax.shard_map(
        body, mesh=mesh, in_specs=placed, out_specs=P("row", "col"), check_vma=False
    )
```

```python
import functools

import jax
import jax.numpy as jnp
from jax import lax
from jax.experimental import pallas as pl
from jax.experimental.pallas import tpu as pltpu
from jax.sharding import PartitionSpec as P

MESH = pl.DeviceIdType.MESH
FIRST, LAST = 4, 4
XN, CR = 2, 3
L = dict(z_own=3, z_relay=1, x_own=4, x_far=-1, x_relay_own=-1, x_relay_near=-1, x_relay_far=-2, c_own=3, c_pair=1, c_near=1, c_near2=0, c_far=0, c_far2=-2, products_c=-3, products_b=-3)
XT = ((-4, -2, 5, 8, 11, 14, 7, 10, 13, 16, 18), (-4, -2, 9, 10, 11, 12, 11, 12, 13, 14, 16))
B_RELAY, B_NEAR, B_FAR, B_SPREAD, B_LAST, B_KINDS = 0, 1, 2, 3, 7, 8
C_PAIR, C_NEAR, C_FAR, C_CORE, C_KINDS = 0, 1, 3, 5, 6
NT = (((1,), (1,)), ((), ()))


def split(v):
    high = v.astype(jnp.bfloat16)
    return high, (v - high.astype(jnp.float32)).astype(jnp.bfloat16)


def kernel(
    w_ref, c_ref, b_ref, scale_ref, out_ref,
    cbuf, bbuf, wfull, whigh, wlow, thigh, tlow, sig, part1, half, part2, turned,
    load_sem, c_recv, b_recv, c_send, b_send, recv1, recv2, send1, send2,
):
    orbitals, states, aux = c_ref.shape
    row, col = lax.axis_index("row"), lax.axis_index("col")
    x, zh = row // 4, row % 4
    y, zl, core = col // 4, (col // 2) % 2, col % 2

    def row_of(x_at, zh_at):
        return (x_at + 4) % 4 * 4 + (zh_at + 4) % 4

    def col_of(y_at, zl_at, core_at):
        return (y_at + 4) % 4 * 4 + zl_at * 2 + core_at

    barrier = pltpu.get_barrier_semaphore()
    for step in range(1, 16):
        pl.semaphore_signal(barrier, inc=1, device_id=(row, (col + step) % 16), device_id_type=MESH)
        pl.semaphore_signal(barrier, inc=1, device_id=((row + step) % 16, col), device_id_type=MESH)

    loads = [
        pltpu.make_async_copy(w_ref, wfull, load_sem.at[0]),
        pltpu.make_async_copy(c_ref, cbuf.at[col], load_sem.at[1]),
        pltpu.make_async_copy(b_ref, bbuf.at[row], load_sem.at[2]),
    ]
    for load in loads:
        load.start()
    sig[...] = jnp.zeros_like(sig)
    pl.semaphore_wait(barrier, 30)

    def c_copy(g, piece, edge, kind, to, own=False):
        return pltpu.make_async_remote_copy(
            src_ref=c_ref.at[g] if own else cbuf.at[piece, g],
            dst_ref=cbuf.at[piece, g],
            send_sem=c_send.at[edge],
            recv_sem=c_recv.at[kind, g],
            device_id=(row, to),
            device_id_type=MESH,
        )

    def b_copy(g, piece, edge, kind, to, own=False):
        return pltpu.make_async_remote_copy(
            src_ref=b_ref.at[g] if own else bbuf.at[piece, g],
            dst_ref=bbuf.at[piece, g],
            send_sem=b_send.at[edge],
            recv_sem=b_recv.at[kind, g],
            device_id=(to, col),
            device_id_type=MESH,
        )

    def got_c(g, kind, pieces=1):
        block = cbuf.at[pl.ds(0, pieces), g]
        pltpu.make_async_copy(block, block, c_recv.at[kind, g]).wait()

    def got_b(g, kind, pieces=1):
        block = bbuf.at[pl.ds(0, pieces), g]
        pltpu.make_async_copy(block, block, b_recv.at[kind, g]).wait()

    def way_of(g):
        return 1 - 2 * (g % 2)

    def z_own(g):
        way = way_of(g)
        b_copy(g, row, 0, B_RELAY, row_of(x, zh + way), True).start()
        b_copy(g, row, 1, B_NEAR, row_of(x, zh - way), True).start()

    def z_relay(g):
        way = way_of(g)
        got_b(g, B_RELAY)
        b_copy(g, row_of(x, zh - way), 4, B_FAR, row_of(x, zh + way)).start()

    def x_own(g):
        way = way_of(g)
        b_copy(g, row, 2, B_SPREAD, row_of(x + way, zh), True).start()
        b_copy(g, row, 3, B_LAST, row_of(x - way, zh), True).start()

    def x_near(g):
        way = way_of(g)
        got_b(g, B_NEAR)
        for at in range(2):
            piece = row_of(x, zh - way + 2 * at * way)
            b_copy(g, piece, 5 + 2 * at, B_SPREAD + 1, row_of(x + way, zh)).start()
            b_copy(g, piece, 6 + 2 * at, B_LAST, row_of(x - way, zh)).start()

    def x_far(g):
        way = way_of(g)
        got_b(g, B_FAR)
        piece = row_of(x, zh + 2)
        b_copy(g, piece, 10, B_SPREAD + 3, row_of(x + way, zh)).start()
        b_copy(g, piece, 11, B_LAST, row_of(x - way, zh)).start()

    def x_relay_own(g):
        way = way_of(g)
        got_b(g, B_SPREAD)
        b_copy(g, row_of(x - way, zh), 9, B_LAST, row_of(x + way, zh)).start()

    def x_relay_near(g):
        way = way_of(g)
        got_b(g, B_SPREAD + 1, 2)
        for at in range(2):
            piece = row_of(x - way, zh - 1 + 2 * at)
            b_copy(g, piece, 12 + at, B_LAST, row_of(x + way, zh)).start()

    def x_relay_far(g):
        way = way_of(g)
        got_b(g, B_SPREAD + 3)
        b_copy(g, row_of(x - way, zh + 2), 14, B_LAST, row_of(x + way, zh)).start()

    def x_offset(at, way):
        return (0, -way, way, 2)[at]

    def first_x_own(g):
        way = way_of(g)
        b_copy(g, row, 0, B_RELAY, row_of(x + way, zh), True).start()
        b_copy(g, row, 1, B_NEAR, row_of(x - way, zh), True).start()

    def first_x_relay(g):
        way = way_of(g)
        got_b(g, B_RELAY)
        b_copy(g, row_of(x - way, zh), 10, B_FAR, row_of(x + way, zh)).start()

    def then_z(g, at, own):
        way = way_of(g)
        piece = row_of(x + x_offset(at, way), zh)
        b_copy(g, piece, 2 + 2 * at, B_SPREAD + at, row_of(x, zh + way), own).start()
        b_copy(g, piece, 3 + 2 * at, B_LAST, row_of(x, zh - way), own).start()

    def then_z_relay(g, at):
        way = way_of(g)
        got_b(g, B_SPREAD + at)
        piece = row_of(x + x_offset(at, way), zh - way)
        b_copy(g, piece, 11 + at, B_LAST, row_of(x, zh + way)).start()

    def c_own(g):
        c_copy(g, col, 0, C_PAIR, col_of(y, 1 - zl, core), True).start()
        c_copy(g, col, 1, C_NEAR, col_of(y + 1, zl, core), True).start()
        c_copy(g, col, 2, C_NEAR, col_of(y - 1, zl, core), True).start()
        c_copy(g, col, 3, C_CORE, col_of(y, zl, 1 - core), True).start()

    def c_pair(g):
        got_c(g, C_PAIR)
        piece = col_of(y, 1 - zl, core)
        c_copy(g, piece, 4, C_NEAR + 1, col_of(y + 1, zl, core)).start()
        c_copy(g, piece, 5, C_NEAR + 1, col_of(y - 1, zl, core)).start()
        c_copy(g, piece, 6, C_CORE, col_of(y, zl, 1 - core)).start()

    def c_spread(g, far):
        way = way_of(g)
        got_c(g, C_NEAR + far, 2)
        zl_at = zl + far - 2 * zl * far
        piece = col_of(y - way, zl_at, core)
        c_copy(g, piece, 7 + far, C_FAR + far, col_of(y + way, zl, core)).start()
        c_copy(g, piece, 9 + far, C_CORE, col_of(y, zl, 1 - core)).start()
        piece = col_of(y + way, zl_at, core)
        c_copy(g, piece, 11 + far, C_CORE, col_of(y, zl, 1 - core)).start()

    def c_far(g, far):
        got_c(g, C_FAR + far)
        piece = col_of(y + 2, zl + far - 2 * zl * far, core)
        c_copy(g, piece, 13 + far, C_CORE, col_of(y, zl, 1 - core)).start()

    def products_c(g):
        got_c(g, C_CORE, 8)
        c_high, c_low = split(cbuf[:, g].reshape(16 * states, aux))
        t = jnp.dot(c_high, whigh[...], preferred_element_type=jnp.float32)
        t += jnp.dot(c_high, wlow[...], preferred_element_type=jnp.float32)
        t += jnp.dot(c_low, whigh[...], preferred_element_type=jnp.float32)
        t_high, t_low = split(t * scale_ref[g])
        thigh[g] = t_high
        tlow[g] = t_low

    def products_b(g):
        got_b(g, B_LAST, 8)
        b_high, b_low = split(bbuf[:, g].reshape(16 * states, aux))
        s = lax.dot_general(b_high, thigh[g], NT, preferred_element_type=jnp.float32)
        s += lax.dot_general(b_high, tlow[g], NT, preferred_element_type=jnp.float32)
        s += lax.dot_general(b_low, thigh[g], NT, preferred_element_type=jnp.float32)
        sig[...] += s

    @pl.loop(0, orbitals + FIRST + LAST)
    def tick(step):
        t = step - FIRST

        def when(g, first, do):
            @pl.when((g >= first) & (g < orbitals))
            def _():
                do(g)

        def c_when(lead, do):
            at = t + lead
            first = at + at // CR

            @pl.when((at >= 0) & (first < orbitals))
            def _():
                do(first)

            @pl.when((at >= 0) & (at % CR == CR - 1) & (first + 1 < orbitals))
            def _():
                do(first + 1)

        def at_tick(ticks, do, *args):
            @pl.when(t == ticks)
            def _():
                do(*args)

        when(t + L["z_own"], XN, z_own)
        for g in range(XN):
            at_tick(XT[g][0], first_x_own, g)
        when(t + L["x_own"], XN, x_own)
        c_when(L["c_own"], c_own)

        @pl.when(step == 0)
        def _():
            for load in loads:
                load.wait()
            w_high, w_low = split(wfull[...])
            whigh[...] = w_high
            wlow[...] = w_low

        when(t + L["z_relay"], XN, z_relay)
        when(t, XN, x_near)
        when(t + L["x_far"], XN, x_far)
        when(t + L["x_relay_own"], XN, x_relay_own)
        when(t + L["x_relay_near"], XN, x_relay_near)
        when(t + L["x_relay_far"], XN, x_relay_far)
        for g in range(XN):
            at_tick(XT[g][1], first_x_relay, g)
            for at in range(4):
                if at == 1:
                    at_tick(XT[g][2 + at], got_b, g, B_NEAR)
                if at == 3:
                    at_tick(XT[g][2 + at], got_b, g, B_FAR)
                at_tick(XT[g][2 + at], then_z, g, at, at == 0)
                at_tick(XT[g][6 + at], then_z_relay, g, at)
        c_when(L["c_pair"], c_pair)
        c_when(L["c_near"], lambda g: c_spread(g, 0))
        c_when(L["c_near2"], lambda g: c_spread(g, 1))
        c_when(L["c_far"], lambda g: c_far(g, 0))
        c_when(L["c_far2"], lambda g: c_far(g, 1))
        c_when(L["products_c"], products_c)
        when(t + L["products_b"], XN, products_b)
        for g in range(XN):
            at_tick(XT[g][10], products_b, g)

    def copy1(step):
        to = (col + step) % 16
        return pltpu.make_async_remote_copy(
            src_ref=sig.at[pl.ds(pl.multiple_of(to * states, states), states)],
            dst_ref=part1.at[col],
            send_sem=send1,
            recv_sem=recv1,
            device_id=(row, to),
            device_id_type=MESH,
        )

    def copy2(step):
        to = (row + step) % 16
        return pltpu.make_async_remote_copy(
            src_ref=half.at[to // 8],
            dst_ref=part2.at[row],
            send_sem=send2,
            recv_sem=recv2,
            device_id=(to, col),
            device_id_type=MESH,
        )

    def wait_all(parts, semaphore):
        others = parts.at[pl.ds(0, 15)]
        pltpu.make_async_copy(others, others, semaphore).wait()

    for step in range(1, 16):
        copy1(step).start()
    part1[col] = sig[pl.ds(pl.multiple_of(col * states, states), states), :]
    wait_all(part1, recv1)
    total = jnp.sum(part1[...], axis=0)
    half[0] = total[:, :128]
    half[1] = total[:, 128:]
    for step in range(1, 16):
        copy2(step).start()
    part2[row] = half[row // 8]
    wait_all(part2, recv2)
    turned[...] = jnp.sum(part2[...], axis=0).T
    out_ref[...] = turned[pl.ds(pl.multiple_of(row % 8 * states, states), states), :]

    wait_all(part1, send1)
    wait_all(part2, send2)
    for edge in range(15):
        pltpu.make_async_copy(c_ref, cbuf.at[0], c_send.at[edge]).wait()
        pltpu.make_async_copy(b_ref, bbuf.at[0], b_send.at[edge]).wait()


def body(screened, fit_coeffs, coulomb_factors, orbital_weights):
    orbitals, aux, states = fit_coeffs.shape
    f32, bf16 = jnp.float32, jnp.bfloat16
    dma = pltpu.SemaphoreType.DMA
    return pl.pallas_call(
        kernel,
        out_shape=jax.ShapeDtypeStruct((states, states), f32),
        in_specs=[pl.BlockSpec(memory_space=pl.ANY)] * 3 + [pl.BlockSpec(memory_space=pltpu.SMEM)],
        out_specs=pl.BlockSpec(memory_space=pltpu.VMEM),
        scratch_shapes=[
            pltpu.VMEM((16, orbitals, states, aux), f32),
            pltpu.VMEM((16, orbitals, states, aux), f32),
            pltpu.VMEM((aux, aux), f32),
            pltpu.VMEM((aux, aux), bf16),
            pltpu.VMEM((aux, aux), bf16),
            pltpu.VMEM((orbitals, 16 * states, aux), bf16),
            pltpu.VMEM((orbitals, 16 * states, aux), bf16),
            pltpu.VMEM((16 * states, 16 * states), f32),
            pltpu.VMEM((16, states, 16 * states), f32),
            pltpu.VMEM((2, states, 128), f32),
            pltpu.VMEM((16, states, 128), f32),
            pltpu.VMEM((128, states), f32),
            dma((3,)),
            dma((C_KINDS, orbitals)),
            dma((B_KINDS, orbitals)),
            dma((15,)),
            dma((15,)),
            dma,
            dma,
            dma,
            dma,
        ],
        compiler_params=pltpu.CompilerParams(
            collective_id=0, has_side_effects=True, vmem_limit_bytes=63 * 1024 * 1024
        ),
        cost_estimate=pl.CostEstimate(flops=20_000_000_000, bytes_accessed=4_000_000, transcendentals=0),
    )(
        screened,
        jnp.transpose(fit_coeffs, (0, 2, 1)),
        jnp.transpose(coulomb_factors, (0, 2, 1)),
        orbital_weights,
    )


def solution(mesh):
    placed = (P("row", "col"), P(None, "row", "col"), P(None, "col", "row"), P())
    return jax.shard_map(
        body, mesh=mesh, in_specs=placed, out_specs=P("row", "col"), check_vma=False
    )
```

```python
import functools

import jax
import jax.numpy as jnp
from jax import lax
from jax.experimental import pallas as pl
from jax.experimental.pallas import tpu as pltpu
from jax.sharding import PartitionSpec as P

MESH = pl.DeviceIdType.MESH
FIRST, LAST = 1, 6
XN, CR, W_AT = 2, 2, 1
L = dict(
    z_own=3, z_relay=1, x_own=6, x_far=-1, x_relay_own=0, x_relay_near=-1, x_relay_far=-3,
    c_own=0, c_pair=-1, c_near=-1, c_near2=-2, c_far=-2, c_far2=-4, products_c=-5, products_b=-5,
)
XT = ((0, 2, 5, 8, 11, 14, 7, 10, 13, 16, 18), (0, 3, 9, 11, 12, 13, 11, 13, 14, 15, 17))
B_RELAY, B_NEAR, B_FAR, B_SPREAD, B_LAST, B_KINDS = 0, 1, 2, 3, 7, 8
C_PAIR, C_NEAR, C_FAR, C_CORE, C_KINDS = 0, 1, 3, 5, 6
NT = (((1,), (1,)), ((), ()))


def split(v):
    high = v.astype(jnp.bfloat16)
    return high, (v - high.astype(jnp.float32)).astype(jnp.bfloat16)


def kernel(
    w_ref, c_ref, b_ref, scale_ref, out_ref,
    cbuf, bbuf, wfull, whigh, wlow, thigh, tlow, sig, part1, half, part2, turned,
    load_sem, c_recv, b_recv, c_send, b_send, recv1, recv2, send1, send2,
):
    orbitals, states, aux = c_ref.shape
    row, col = lax.axis_index("row"), lax.axis_index("col")
    x, zh = row // 4, row % 4
    y, zl, core = col // 4, (col // 2) % 2, col % 2

    def row_of(x_at, zh_at):
        return (x_at + 4) % 4 * 4 + (zh_at + 4) % 4

    def col_of(y_at, zl_at, core_at):
        return (y_at + 4) % 4 * 4 + zl_at * 2 + core_at

    barrier = pltpu.get_barrier_semaphore()
    for step in range(1, 16):
        pl.semaphore_signal(barrier, inc=1, device_id=(row, (col + step) % 16), device_id_type=MESH)
        pl.semaphore_signal(barrier, inc=1, device_id=((row + step) % 16, col), device_id_type=MESH)

    loads = [
        pltpu.make_async_copy(w_ref, wfull, load_sem.at[0]),
        pltpu.make_async_copy(c_ref, cbuf.at[col], load_sem.at[1]),
        pltpu.make_async_copy(b_ref, bbuf.at[row], load_sem.at[2]),
    ]
    for load in loads:
        load.start()
    sig[...] = jnp.zeros_like(sig)
    pl.semaphore_wait(barrier, 30)

    def c_copy(g, piece, kind, to, own=False):
        return pltpu.make_async_remote_copy(
            src_ref=c_ref.at[g] if own else cbuf.at[piece, g],
            dst_ref=cbuf.at[piece, g],
            send_sem=c_send,
            recv_sem=c_recv.at[kind, g],
            device_id=(row, to),
            device_id_type=MESH,
        )

    def b_copy(g, piece, kind, to, own=False):
        return pltpu.make_async_remote_copy(
            src_ref=b_ref.at[g] if own else bbuf.at[piece, g],
            dst_ref=bbuf.at[piece, g],
            send_sem=b_send,
            recv_sem=b_recv.at[kind, g],
            device_id=(to, col),
            device_id_type=MESH,
        )

    def got_c(g, kind, pieces=1):
        block = cbuf.at[pl.ds(0, pieces), g]
        pltpu.make_async_copy(block, block, c_recv.at[kind, g]).wait()

    def got_b(g, kind, pieces=1):
        block = bbuf.at[pl.ds(0, pieces), g]
        pltpu.make_async_copy(block, block, b_recv.at[kind, g]).wait()

    def way_of(g):
        return 1 - 2 * (g % 2)

    def z_own(g):
        way = way_of(g)
        b_copy(g, row, B_RELAY, row_of(x, zh + way), True).start()
        b_copy(g, row, B_NEAR, row_of(x, zh - way), True).start()

    def z_relay(g):
        way = way_of(g)
        got_b(g, B_RELAY)
        b_copy(g, row_of(x, zh - way), B_FAR, row_of(x, zh + way)).start()

    def x_own(g):
        way = way_of(g)
        b_copy(g, row, B_SPREAD, row_of(x + way, zh), True).start()
        b_copy(g, row, B_LAST, row_of(x - way, zh), True).start()

    def x_near(g):
        way = way_of(g)
        got_b(g, B_NEAR)
        for at in range(2):
            piece = row_of(x, zh - way + 2 * at * way)
            b_copy(g, piece, B_SPREAD + 1, row_of(x + way, zh)).start()
            b_copy(g, piece, B_LAST, row_of(x - way, zh)).start()

    def x_far(g):
        way = way_of(g)
        got_b(g, B_FAR)
        piece = row_of(x, zh + 2)
        b_copy(g, piece, B_SPREAD + 3, row_of(x + way, zh)).start()
        b_copy(g, piece, B_LAST, row_of(x - way, zh)).start()

    def x_relay_own(g):
        way = way_of(g)
        got_b(g, B_SPREAD)
        b_copy(g, row_of(x - way, zh), B_LAST, row_of(x + way, zh)).start()

    def x_relay_near(g):
        way = way_of(g)
        got_b(g, B_SPREAD + 1, 2)
        for at in range(2):
            piece = row_of(x - way, zh - 1 + 2 * at)
            b_copy(g, piece, B_LAST, row_of(x + way, zh)).start()

    def x_relay_far(g):
        way = way_of(g)
        got_b(g, B_SPREAD + 3)
        b_copy(g, row_of(x - way, zh + 2), B_LAST, row_of(x + way, zh)).start()

    def x_offset(at, way):
        return (0, -way, way, 2)[at]

    def first_x_own(g):
        way = way_of(g)
        b_copy(g, row, B_RELAY, row_of(x + way, zh), True).start()
        b_copy(g, row, B_NEAR, row_of(x - way, zh), True).start()

    def first_x_relay(g):
        way = way_of(g)
        got_b(g, B_RELAY)
        b_copy(g, row_of(x - way, zh), B_FAR, row_of(x + way, zh)).start()

    def then_z(g, at, own):
        way = way_of(g)
        piece = row_of(x + x_offset(at, way), zh)
        b_copy(g, piece, B_SPREAD + at, row_of(x, zh + way), own).start()
        b_copy(g, piece, B_LAST, row_of(x, zh - way), own).start()

    def then_z_relay(g, at):
        way = way_of(g)
        got_b(g, B_SPREAD + at)
        piece = row_of(x + x_offset(at, way), zh - way)
        b_copy(g, piece, B_LAST, row_of(x, zh + way)).start()

    def c_own(g):
        c_copy(g, col, C_PAIR, col_of(y, 1 - zl, core), True).start()
        c_copy(g, col, C_NEAR, col_of(y + 1, zl, core), True).start()
        c_copy(g, col, C_NEAR, col_of(y - 1, zl, core), True).start()
        c_copy(g, col, C_CORE, col_of(y, zl, 1 - core), True).start()

    def c_pair(g):
        got_c(g, C_PAIR)
        piece = col_of(y, 1 - zl, core)
        c_copy(g, piece, C_NEAR + 1, col_of(y + 1, zl, core)).start()
        c_copy(g, piece, C_NEAR + 1, col_of(y - 1, zl, core)).start()
        c_copy(g, piece, C_CORE, col_of(y, zl, 1 - core)).start()

    def c_spread(g, far):
        way = way_of(g)
        got_c(g, C_NEAR + far, 2)
        zl_at = zl + far - 2 * zl * far
        piece = col_of(y - way, zl_at, core)
        c_copy(g, piece, C_FAR + far, col_of(y + way, zl, core)).start()
        c_copy(g, piece, C_CORE, col_of(y, zl, 1 - core)).start()
        piece = col_of(y + way, zl_at, core)
        c_copy(g, piece, C_CORE, col_of(y, zl, 1 - core)).start()

    def c_far(g, far):
        got_c(g, C_FAR + far)
        piece = col_of(y + 2, zl + far - 2 * zl * far, core)
        c_copy(g, piece, C_CORE, col_of(y, zl, 1 - core)).start()

    def products_c(g):
        got_c(g, C_CORE, 8)
        c_high, c_low = split(cbuf[:, g].reshape(16 * states, aux))
        t = jnp.dot(c_high, whigh[...], preferred_element_type=jnp.float32)
        t += jnp.dot(c_high, wlow[...], preferred_element_type=jnp.float32)
        t += jnp.dot(c_low, whigh[...], preferred_element_type=jnp.float32)
        t_high, t_low = split(t * scale_ref[g])
        thigh[g] = t_high
        tlow[g] = t_low

    def products_b(g):
        got_b(g, B_LAST, 8)
        b_high, b_low = split(bbuf[:, g].reshape(16 * states, aux))
        s = lax.dot_general(b_high, thigh[g], NT, preferred_element_type=jnp.float32)
        s += lax.dot_general(b_high, tlow[g], NT, preferred_element_type=jnp.float32)
        s += lax.dot_general(b_low, thigh[g], NT, preferred_element_type=jnp.float32)
        sig[...] += s

    z_own(XN)
    for g in range(XN):
        first_x_own(g)
    for g in range(XN + 1, FIRST + L["z_own"]):
        z_own(g)
    for g in range(XN, FIRST + L["x_own"]):
        x_own(g)
    for at in range(FIRST + L["c_own"]):
        c_own(at + at // CR)

    @pl.loop(FIRST, orbitals + LAST)
    def tick(t):
        def when(g, first, do):
            @pl.when((g >= first) & (g < orbitals))
            def _():
                do(g)

        def c_when(lead, do):
            at = t + lead
            first = at + at // CR

            @pl.when((at >= 0) & (first < orbitals))
            def _():
                do(first)

            @pl.when((at >= 0) & (at % CR == CR - 1) & (first + 1 < orbitals))
            def _():
                do(first + 1)

        def at_tick(ticks, do, *args):
            @pl.when(t == ticks)
            def _():
                do(*args)

        when(t + L["z_own"], XN, z_own)
        when(t + L["x_own"], XN, x_own)
        c_when(L["c_own"], c_own)

        when(t + L["z_relay"], XN, z_relay)
        when(t, XN, x_near)
        when(t + L["x_far"], XN, x_far)
        when(t + L["x_relay_own"], XN, x_relay_own)
        when(t + L["x_relay_near"], XN, x_relay_near)
        when(t + L["x_relay_far"], XN, x_relay_far)
        for g in range(XN):
            at_tick(XT[g][1], first_x_relay, g)
            for at in range(4):
                if at == 1:
                    at_tick(XT[g][2 + at], got_b, g, B_NEAR)
                if at == 3:
                    at_tick(XT[g][2 + at], got_b, g, B_FAR)
                at_tick(XT[g][2 + at], then_z, g, at, at == 0)
                at_tick(XT[g][6 + at], then_z_relay, g, at)
        @pl.when(t == W_AT)
        def _():
            for load in loads:
                load.wait()
            w_high, w_low = split(wfull[...])
            whigh[...] = w_high
            wlow[...] = w_low

        c_when(L["c_pair"], c_pair)
        c_when(L["c_near"], lambda g: c_spread(g, 0))
        c_when(L["c_near2"], lambda g: c_spread(g, 1))
        c_when(L["c_far"], lambda g: c_far(g, 0))
        c_when(L["c_far2"], lambda g: c_far(g, 1))
        c_when(L["products_c"], products_c)
        when(t + L["products_b"], XN, products_b)
        for g in range(XN):
            at_tick(XT[g][10], products_b, g)

    def copy1(step):
        to = (col + step) % 16
        return pltpu.make_async_remote_copy(
            src_ref=sig.at[pl.ds(pl.multiple_of(to * states, states), states)],
            dst_ref=part1.at[col],
            send_sem=send1,
            recv_sem=recv1,
            device_id=(row, to),
            device_id_type=MESH,
        )

    def copy2(step):
        to = (row + step) % 16
        return pltpu.make_async_remote_copy(
            src_ref=half.at[to // 8],
            dst_ref=part2.at[row],
            send_sem=send2,
            recv_sem=recv2,
            device_id=(to, col),
            device_id_type=MESH,
        )

    def wait_all(parts, semaphore):
        others = parts.at[pl.ds(0, 15)]
        pltpu.make_async_copy(others, others, semaphore).wait()

    for step in range(1, 16):
        copy1(step).start()
    part1[col] = sig[pl.ds(pl.multiple_of(col * states, states), states), :]
    wait_all(part1, recv1)
    total = jnp.sum(part1[...], axis=0)
    half[0] = total[:, :128]
    half[1] = total[:, 128:]
    for step in range(1, 16):
        copy2(step).start()
    part2[row] = half[row // 8]
    wait_all(part2, recv2)
    turned[...] = jnp.sum(part2[...], axis=0).T
    out_ref[...] = turned[pl.ds(pl.multiple_of(row % 8 * states, states), states), :]

    wait_all(part1, send1)
    wait_all(part2, send2)
    wait_all(cbuf, c_send)
    wait_all(bbuf, b_send)


def body(screened, fit_coeffs, coulomb_factors, orbital_weights):
    orbitals, aux, states = fit_coeffs.shape
    f32, bf16 = jnp.float32, jnp.bfloat16
    dma = pltpu.SemaphoreType.DMA
    return pl.pallas_call(
        kernel,
        out_shape=jax.ShapeDtypeStruct((states, states), f32),
        in_specs=[pl.BlockSpec(memory_space=pl.ANY)] * 3 + [pl.BlockSpec(memory_space=pltpu.SMEM)],
        out_specs=pl.BlockSpec(memory_space=pltpu.VMEM),
        scratch_shapes=[
            pltpu.VMEM((16, orbitals, states, aux), f32),
            pltpu.VMEM((16, orbitals, states, aux), f32),
            pltpu.VMEM((aux, aux), f32),
            pltpu.VMEM((aux, aux), bf16),
            pltpu.VMEM((aux, aux), bf16),
            pltpu.VMEM((orbitals, 16 * states, aux), bf16),
            pltpu.VMEM((orbitals, 16 * states, aux), bf16),
            pltpu.VMEM((16 * states, 16 * states), f32),
            pltpu.VMEM((16, states, 16 * states), f32),
            pltpu.VMEM((2, states, 128), f32),
            pltpu.VMEM((16, states, 128), f32),
            pltpu.VMEM((128, states), f32),
            dma((3,)),
            dma((C_KINDS, orbitals)),
            dma((B_KINDS, orbitals)),
            dma,
            dma,
            dma,
            dma,
            dma,
            dma,
        ],
        compiler_params=pltpu.CompilerParams(
            collective_id=0, has_side_effects=True, vmem_limit_bytes=63 * 1024 * 1024
        ),
        cost_estimate=pl.CostEstimate(flops=20_000_000_000, bytes_accessed=4_000_000, transcendentals=0),
    )(
        screened,
        jnp.transpose(fit_coeffs, (0, 2, 1)),
        jnp.transpose(coulomb_factors, (0, 2, 1)),
        orbital_weights,
    )


def solution(mesh):
    placed = (P("row", "col"), P(None, "row", "col"), P(None, "col", "row"), P())
    return jax.shard_map(
        body, mesh=mesh, in_specs=placed, out_specs=P("row", "col"), check_vma=False
    )
```

```python
import functools

import jax
import jax.numpy as jnp
from jax import lax
from jax.experimental import pallas as pl
from jax.experimental.pallas import tpu as pltpu
from jax.sharding import PartitionSpec as P

MESH = pl.DeviceIdType.MESH
FIRST, LAST = 1, 5
XN, CR, W_AT = 2, 2, 1
L = dict(
    z_own=3, z_relay=1, x_own=6, x_far=-1, x_relay_own=0, x_relay_near=-1, x_relay_far=-2,
    c_own=0, c_pair=-1, c_near=-1, c_near2=-2, c_far=-2, c_far2=-3, products_c=-5, products_b=-4,
)
XT = ((0, 2, 5, 8, 11, 14, 7, 10, 13, 16, 18), (0, 3, 9, 11, 12, 13, 11, 13, 14, 15, 17))
B_RELAY, B_NEAR, B_FAR, B_SPREAD, B_LAST, B_KINDS = 0, 1, 2, 3, 7, 8
C_PAIR, C_NEAR, C_FAR, C_CORE, C_KINDS = 0, 1, 3, 5, 6
NT = (((1,), (1,)), ((), ()))


def split(v):
    high = v.astype(jnp.bfloat16)
    return high, (v - high.astype(jnp.float32)).astype(jnp.bfloat16)


def kernel(
    w_ref, c_ref, b_ref, scale_ref, out_ref,
    cbuf, bbuf, wfull, whigh, wlow, thigh, tlow, sig, part1, half, part2, turned,
    load_sem, c_recv, b_recv, c_send, b_send, recv1, recv2, send1, send2,
):
    orbitals, states, aux = c_ref.shape
    row, col = lax.axis_index("row"), lax.axis_index("col")
    x, zh = row // 4, row % 4
    y, zl, core = col // 4, (col // 2) % 2, col % 2

    def row_of(x_at, zh_at):
        return (x_at + 4) % 4 * 4 + (zh_at + 4) % 4

    def col_of(y_at, zl_at, core_at):
        return (y_at + 4) % 4 * 4 + zl_at * 2 + core_at

    barrier = pltpu.get_barrier_semaphore()
    for step in range(1, 16):
        pl.semaphore_signal(barrier, inc=1, device_id=(row, (col + step) % 16), device_id_type=MESH)
        pl.semaphore_signal(barrier, inc=1, device_id=((row + step) % 16, col), device_id_type=MESH)

    loads = [
        pltpu.make_async_copy(w_ref, wfull, load_sem.at[0]),
        pltpu.make_async_copy(c_ref, cbuf.at[col], load_sem.at[1]),
        pltpu.make_async_copy(b_ref, bbuf.at[row], load_sem.at[2]),
    ]
    for load in loads:
        load.start()
    sig[...] = jnp.zeros_like(sig)
    pl.semaphore_wait(barrier, 30)

    def c_copy(g, piece, kind, to, own=False):
        return pltpu.make_async_remote_copy(
            src_ref=c_ref.at[g] if own else cbuf.at[piece, g],
            dst_ref=cbuf.at[piece, g],
            send_sem=c_send,
            recv_sem=c_recv.at[kind, g],
            device_id=(row, to),
            device_id_type=MESH,
        )

    def b_copy(g, piece, kind, to, own=False):
        return pltpu.make_async_remote_copy(
            src_ref=b_ref.at[g] if own else bbuf.at[piece, g],
            dst_ref=bbuf.at[piece, g],
            send_sem=b_send,
            recv_sem=b_recv.at[kind, g],
            device_id=(to, col),
            device_id_type=MESH,
        )

    def got_c(g, kind, pieces=1):
        block = cbuf.at[pl.ds(0, pieces), g]
        pltpu.make_async_copy(block, block, c_recv.at[kind, g]).wait()

    def got_b(g, kind, pieces=1):
        block = bbuf.at[pl.ds(0, pieces), g]
        pltpu.make_async_copy(block, block, b_recv.at[kind, g]).wait()

    def way_of(g):
        return 1 - 2 * (g % 2)

    def z_own(g):
        way = way_of(g)
        b_copy(g, row, B_RELAY, row_of(x, zh + way), True).start()
        b_copy(g, row, B_NEAR, row_of(x, zh - way), True).start()

    def z_relay(g):
        way = way_of(g)
        got_b(g, B_RELAY)
        b_copy(g, row_of(x, zh - way), B_FAR, row_of(x, zh + way)).start()

    def x_own(g):
        way = way_of(g)
        b_copy(g, row, B_SPREAD, row_of(x + way, zh), True).start()
        b_copy(g, row, B_LAST, row_of(x - way, zh), True).start()

    def x_near(g):
        way = way_of(g)
        got_b(g, B_NEAR)
        for at in range(2):
            piece = row_of(x, zh - way + 2 * at * way)
            b_copy(g, piece, B_SPREAD + 1, row_of(x + way, zh)).start()
            b_copy(g, piece, B_LAST, row_of(x - way, zh)).start()

    def x_far(g):
        way = way_of(g)
        got_b(g, B_FAR)
        piece = row_of(x, zh + 2)
        b_copy(g, piece, B_SPREAD + 3, row_of(x + way, zh)).start()
        b_copy(g, piece, B_LAST, row_of(x - way, zh)).start()

    def x_relay_own(g):
        way = way_of(g)
        got_b(g, B_SPREAD)
        b_copy(g, row_of(x - way, zh), B_LAST, row_of(x + way, zh)).start()

    def x_relay_near(g):
        way = way_of(g)
        got_b(g, B_SPREAD + 1, 2)
        for at in range(2):
            piece = row_of(x - way, zh - 1 + 2 * at)
            b_copy(g, piece, B_LAST, row_of(x + way, zh)).start()

    def x_relay_far(g):
        way = way_of(g)
        got_b(g, B_SPREAD + 3)
        b_copy(g, row_of(x - way, zh + 2), B_LAST, row_of(x + way, zh)).start()

    def x_offset(at, way):
        return (0, -way, way, 2)[at]

    def first_x_own(g):
        way = way_of(g)
        b_copy(g, row, B_RELAY, row_of(x + way, zh), True).start()
        b_copy(g, row, B_NEAR, row_of(x - way, zh), True).start()

    def first_x_relay(g):
        way = way_of(g)
        got_b(g, B_RELAY)
        b_copy(g, row_of(x - way, zh), B_FAR, row_of(x + way, zh)).start()

    def then_z(g, at, own):
        way = way_of(g)
        piece = row_of(x + x_offset(at, way), zh)
        b_copy(g, piece, B_SPREAD + at, row_of(x, zh + way), own).start()
        b_copy(g, piece, B_LAST, row_of(x, zh - way), own).start()

    def then_z_relay(g, at):
        way = way_of(g)
        got_b(g, B_SPREAD + at)
        piece = row_of(x + x_offset(at, way), zh - way)
        b_copy(g, piece, B_LAST, row_of(x, zh + way)).start()

    def c_own(g):
        c_copy(g, col, C_PAIR, col_of(y, 1 - zl, core), True).start()
        c_copy(g, col, C_NEAR, col_of(y + 1, zl, core), True).start()
        c_copy(g, col, C_NEAR, col_of(y - 1, zl, core), True).start()
        c_copy(g, col, C_CORE, col_of(y, zl, 1 - core), True).start()

    def c_pair(g):
        got_c(g, C_PAIR)
        piece = col_of(y, 1 - zl, core)
        c_copy(g, piece, C_NEAR + 1, col_of(y + 1, zl, core)).start()
        c_copy(g, piece, C_NEAR + 1, col_of(y - 1, zl, core)).start()
        c_copy(g, piece, C_CORE, col_of(y, zl, 1 - core)).start()

    def c_spread(g, far):
        way = way_of(g)
        got_c(g, C_NEAR + far, 2)
        zl_at = zl + far - 2 * zl * far
        piece = col_of(y - way, zl_at, core)
        c_copy(g, piece, C_FAR + far, col_of(y + way, zl, core)).start()
        c_copy(g, piece, C_CORE, col_of(y, zl, 1 - core)).start()
        piece = col_of(y + way, zl_at, core)
        c_copy(g, piece, C_CORE, col_of(y, zl, 1 - core)).start()

    def c_far(g, far):
        got_c(g, C_FAR + far)
        piece = col_of(y + 2, zl + far - 2 * zl * far, core)
        c_copy(g, piece, C_CORE, col_of(y, zl, 1 - core)).start()

    def products_c(g):
        got_c(g, C_CORE, 8)
        c_high, c_low = split(cbuf[:, g].reshape(16 * states, aux))
        t = jnp.dot(c_high, whigh[...], preferred_element_type=jnp.float32)
        t += jnp.dot(c_high, wlow[...], preferred_element_type=jnp.float32)
        t += jnp.dot(c_low, whigh[...], preferred_element_type=jnp.float32)
        t_high, t_low = split(t * scale_ref[g])
        thigh[g] = t_high
        tlow[g] = t_low

    def products_b(g):
        got_b(g, B_LAST, 8)
        b_high, b_low = split(bbuf[:, g].reshape(16 * states, aux))
        s = lax.dot_general(b_high, thigh[g], NT, preferred_element_type=jnp.float32)
        s += lax.dot_general(b_high, tlow[g], NT, preferred_element_type=jnp.float32)
        s += lax.dot_general(b_low, thigh[g], NT, preferred_element_type=jnp.float32)
        sig[...] += s

    z_own(XN)
    for g in range(XN):
        first_x_own(g)
    for g in range(XN + 1, FIRST + L["z_own"]):
        z_own(g)
    for g in range(XN, FIRST + L["x_own"]):
        x_own(g)
    for at in range(FIRST + L["c_own"]):
        c_own(at + at // CR)

    @pl.loop(FIRST, orbitals + LAST)
    def tick(t):
        def when(g, first, do):
            @pl.when((g >= first) & (g < orbitals))
            def _():
                do(g)

        def c_when(lead, do):
            at = t + lead
            first = at + at // CR

            @pl.when((at >= 0) & (first < orbitals))
            def _():
                do(first)

            @pl.when((at >= 0) & (at % CR == CR - 1) & (first + 1 < orbitals))
            def _():
                do(first + 1)

        def at_tick(ticks, do, *args):
            @pl.when(t == ticks)
            def _():
                do(*args)

        when(t + L["z_own"], XN, z_own)
        when(t + L["x_own"], XN, x_own)
        c_when(L["c_own"], c_own)

        when(t + L["z_relay"], XN, z_relay)
        when(t, XN, x_near)
        when(t + L["x_far"], XN, x_far)
        when(t + L["x_relay_own"], XN, x_relay_own)
        when(t + L["x_relay_near"], XN, x_relay_near)
        when(t + L["x_relay_far"], XN, x_relay_far)
        for g in range(XN):
            at_tick(XT[g][1], first_x_relay, g)
            for at in range(4):
                if at == 1:
                    at_tick(XT[g][2 + at], got_b, g, B_NEAR)
                if at == 3:
                    at_tick(XT[g][2 + at], got_b, g, B_FAR)
                at_tick(XT[g][2 + at], then_z, g, at, at == 0)
                at_tick(XT[g][6 + at], then_z_relay, g, at)
        @pl.when(t == W_AT)
        def _():
            for load in loads:
                load.wait()
            w_high, w_low = split(wfull[...])
            whigh[...] = w_high
            wlow[...] = w_low

        c_when(L["c_pair"], c_pair)
        c_when(L["c_near"], lambda g: c_spread(g, 0))
        c_when(L["c_near2"], lambda g: c_spread(g, 1))
        c_when(L["c_far"], lambda g: c_far(g, 0))
        c_when(L["c_far2"], lambda g: c_far(g, 1))
        c_when(L["products_c"], products_c)
        when(t + L["products_b"], XN, products_b)
        for g in range(XN):
            at_tick(XT[g][10], products_b, g)

    def copy1(step):
        to = (col + step) % 16
        return pltpu.make_async_remote_copy(
            src_ref=sig.at[pl.ds(pl.multiple_of(to * states, states), states)],
            dst_ref=part1.at[col],
            send_sem=send1,
            recv_sem=recv1,
            device_id=(row, to),
            device_id_type=MESH,
        )

    def copy2(step):
        to = (row + step) % 16
        return pltpu.make_async_remote_copy(
            src_ref=half.at[to // 8],
            dst_ref=part2.at[row],
            send_sem=send2,
            recv_sem=recv2,
            device_id=(to, col),
            device_id_type=MESH,
        )

    def wait_all(parts, semaphore):
        others = parts.at[pl.ds(0, 15)]
        pltpu.make_async_copy(others, others, semaphore).wait()

    for step in range(1, 16):
        copy1(step).start()
    part1[col] = sig[pl.ds(pl.multiple_of(col * states, states), states), :]
    wait_all(part1, recv1)
    total = jnp.sum(part1[...], axis=0)
    half[0] = total[:, :128]
    half[1] = total[:, 128:]
    for step in range(1, 16):
        copy2(step).start()
    part2[row] = half[row // 8]
    wait_all(part2, recv2)
    turned[...] = jnp.sum(part2[...], axis=0).T
    out_ref[...] = turned[pl.ds(pl.multiple_of(row % 8 * states, states), states), :]

    wait_all(part1, send1)
    wait_all(part2, send2)
    wait_all(cbuf, c_send)
    wait_all(bbuf, b_send)


def body(screened, fit_coeffs, coulomb_factors, orbital_weights):
    orbitals, aux, states = fit_coeffs.shape
    f32, bf16 = jnp.float32, jnp.bfloat16
    dma = pltpu.SemaphoreType.DMA
    return pl.pallas_call(
        kernel,
        out_shape=jax.ShapeDtypeStruct((states, states), f32),
        in_specs=[pl.BlockSpec(memory_space=pl.ANY)] * 3 + [pl.BlockSpec(memory_space=pltpu.SMEM)],
        out_specs=pl.BlockSpec(memory_space=pltpu.VMEM),
        scratch_shapes=[
            pltpu.VMEM((16, orbitals, states, aux), f32),
            pltpu.VMEM((16, orbitals, states, aux), f32),
            pltpu.VMEM((aux, aux), f32),
            pltpu.VMEM((aux, aux), bf16),
            pltpu.VMEM((aux, aux), bf16),
            pltpu.VMEM((orbitals, 16 * states, aux), bf16),
            pltpu.VMEM((orbitals, 16 * states, aux), bf16),
            pltpu.VMEM((16 * states, 16 * states), f32),
            pltpu.VMEM((16, states, 16 * states), f32),
            pltpu.VMEM((2, states, 128), f32),
            pltpu.VMEM((16, states, 128), f32),
            pltpu.VMEM((128, states), f32),
            dma((3,)),
            dma((C_KINDS, orbitals)),
            dma((B_KINDS, orbitals)),
            dma,
            dma,
            dma,
            dma,
            dma,
            dma,
        ],
        compiler_params=pltpu.CompilerParams(
            collective_id=0, has_side_effects=True, vmem_limit_bytes=63 * 1024 * 1024
        ),
        cost_estimate=pl.CostEstimate(flops=20_000_000_000, bytes_accessed=4_000_000, transcendentals=0),
    )(
        screened,
        jnp.transpose(fit_coeffs, (0, 2, 1)),
        jnp.transpose(coulomb_factors, (0, 2, 1)),
        orbital_weights,
    )


def solution(mesh):
    placed = (P("row", "col"), P(None, "row", "col"), P(None, "col", "row"), P())
    return jax.shard_map(
        body, mesh=mesh, in_specs=placed, out_specs=P("row", "col"), check_vma=False
    )
```

```python
import functools

import jax
import jax.numpy as jnp
from jax import lax
from jax.experimental import pallas as pl
from jax.experimental.pallas import tpu as pltpu
from jax.sharding import PartitionSpec as P

MESH = pl.DeviceIdType.MESH
FIRST, LAST = 1, 5
XN, CR, W_AT = 2, 2, 1
L = dict(
    z_own=3, z_relay=1, x_own=6, x_far=-1, x_relay_own=0, x_relay_near=-1, x_relay_far=-2,
    c_own=0, c_pair=-1, c_near=-1, c_near2=-2, c_far=-2, c_far2=-3, products_c=-5, products_b=-4,
)
XT = ((0, 2, 5, 8, 11, 14, 7, 10, 13, 16, 18), (0, 3, 9, 11, 12, 13, 11, 13, 14, 15, 17))
B_RELAY, B_NEAR, B_FAR, B_SPREAD, B_LAST, B_KINDS = 0, 1, 2, 3, 7, 8
C_PAIR, C_NEAR, C_FAR, C_CORE, C_KINDS = 0, 1, 3, 5, 6
NT = (((1,), (1,)), ((), ()))


def split(v):
    high = v.astype(jnp.bfloat16)
    return high, (v - high.astype(jnp.float32)).astype(jnp.bfloat16)


def kernel(
    w_ref, c_ref, b_ref, scale_ref, out_ref,
    cbuf, bbuf, wfull, whigh, wlow, thigh, tlow, sig, part1, half, part2, turned,
    load_sem, c_recv, b_recv, c_send, b_send, recv1, recv2, send1, send2,
):
    orbitals, states, aux = c_ref.shape
    row, col = lax.axis_index("row"), lax.axis_index("col")
    x, zh = row // 4, row % 4
    y, zl, core = col // 4, (col // 2) % 2, col % 2

    def row_of(x_at, zh_at):
        return (x_at + 4) % 4 * 4 + (zh_at + 4) % 4

    def col_of(y_at, zl_at, core_at):
        return (y_at + 4) % 4 * 4 + zl_at * 2 + core_at

    barrier = pltpu.get_barrier_semaphore()
    for step in range(1, 16):
        pl.semaphore_signal(barrier, inc=1, device_id=(row, (col + step) % 16), device_id_type=MESH)
        pl.semaphore_signal(barrier, inc=1, device_id=((row + step) % 16, col), device_id_type=MESH)

    loads = [
        pltpu.make_async_copy(w_ref, wfull, load_sem.at[0]),
        pltpu.make_async_copy(c_ref, cbuf.at[col], load_sem.at[1]),
        pltpu.make_async_copy(b_ref, bbuf.at[row], load_sem.at[2]),
    ]
    for load in loads:
        load.start()
    sig[...] = jnp.zeros_like(sig)
    pl.semaphore_wait(barrier, 30)

    def c_copy(g, piece, kind, to, own=False):
        return pltpu.make_async_remote_copy(
            src_ref=c_ref.at[g] if own else cbuf.at[piece, g],
            dst_ref=cbuf.at[piece, g],
            send_sem=c_send,
            recv_sem=c_recv.at[kind, g],
            device_id=(row, to),
            device_id_type=MESH,
        )

    def b_copy(g, piece, kind, to, own=False):
        return pltpu.make_async_remote_copy(
            src_ref=b_ref.at[g] if own else bbuf.at[piece, g],
            dst_ref=bbuf.at[piece, g],
            send_sem=b_send,
            recv_sem=b_recv.at[kind, g],
            device_id=(to, col),
            device_id_type=MESH,
        )

    def got_c(g, kind, pieces=1):
        block = cbuf.at[pl.ds(0, pieces), g]
        pltpu.make_async_copy(block, block, c_recv.at[kind, g]).wait()

    def got_b(g, kind, pieces=1):
        block = bbuf.at[pl.ds(0, pieces), g]
        pltpu.make_async_copy(block, block, b_recv.at[kind, g]).wait()

    def way_of(g):
        return 1 - 2 * (g % 2)

    def z_own(g):
        way = way_of(g)
        b_copy(g, row, B_RELAY, row_of(x, zh + way), True).start()
        b_copy(g, row, B_NEAR, row_of(x, zh - way), True).start()

    def z_relay(g):
        way = way_of(g)
        got_b(g, B_RELAY)
        b_copy(g, row_of(x, zh - way), B_FAR, row_of(x, zh + way)).start()

    def x_own(g):
        way = way_of(g)
        b_copy(g, row, B_SPREAD, row_of(x + way, zh), True).start()
        b_copy(g, row, B_LAST, row_of(x - way, zh), True).start()

    def x_near(g):
        way = way_of(g)
        got_b(g, B_NEAR)
        for at in range(2):
            piece = row_of(x, zh - way + 2 * at * way)
            b_copy(g, piece, B_SPREAD + 1, row_of(x + way, zh)).start()
            b_copy(g, piece, B_LAST, row_of(x - way, zh)).start()

    def x_far(g):
        way = way_of(g)
        got_b(g, B_FAR)
        piece = row_of(x, zh + 2)
        b_copy(g, piece, B_SPREAD + 3, row_of(x + way, zh)).start()
        b_copy(g, piece, B_LAST, row_of(x - way, zh)).start()

    def x_relay_own(g):
        way = way_of(g)
        got_b(g, B_SPREAD)
        b_copy(g, row_of(x - way, zh), B_LAST, row_of(x + way, zh)).start()

    def x_relay_near(g):
        way = way_of(g)
        got_b(g, B_SPREAD + 1, 2)
        for at in range(2):
            piece = row_of(x - way, zh - 1 + 2 * at)
            b_copy(g, piece, B_LAST, row_of(x + way, zh)).start()

    def x_relay_far(g):
        way = way_of(g)
        got_b(g, B_SPREAD + 3)
        b_copy(g, row_of(x - way, zh + 2), B_LAST, row_of(x + way, zh)).start()

    def x_offset(at, way):
        return (0, -way, way, 2)[at]

    def first_x_own(g):
        way = way_of(g)
        b_copy(g, row, B_RELAY, row_of(x + way, zh), True).start()
        b_copy(g, row, B_NEAR, row_of(x - way, zh), True).start()

    def first_x_relay(g):
        way = way_of(g)
        got_b(g, B_RELAY)
        b_copy(g, row_of(x - way, zh), B_FAR, row_of(x + way, zh)).start()

    def then_z(g, at, own):
        way = way_of(g)
        piece = row_of(x + x_offset(at, way), zh)
        b_copy(g, piece, B_SPREAD + at, row_of(x, zh + way), own).start()
        b_copy(g, piece, B_LAST, row_of(x, zh - way), own).start()

    def then_z_relay(g, at):
        way = way_of(g)
        got_b(g, B_SPREAD + at)
        piece = row_of(x + x_offset(at, way), zh - way)
        b_copy(g, piece, B_LAST, row_of(x, zh + way)).start()

    def c_own(g):
        c_copy(g, col, C_PAIR, col_of(y, 1 - zl, core), True).start()
        c_copy(g, col, C_NEAR, col_of(y + 1, zl, core), True).start()
        c_copy(g, col, C_NEAR, col_of(y - 1, zl, core), True).start()
        c_copy(g, col, C_CORE, col_of(y, zl, 1 - core), True).start()

    def c_pair(g):
        got_c(g, C_PAIR)
        piece = col_of(y, 1 - zl, core)
        c_copy(g, piece, C_NEAR + 1, col_of(y + 1, zl, core)).start()
        c_copy(g, piece, C_NEAR + 1, col_of(y - 1, zl, core)).start()
        c_copy(g, piece, C_CORE, col_of(y, zl, 1 - core)).start()

    def c_spread(g, far):
        way = way_of(g)
        got_c(g, C_NEAR + far, 2)
        zl_at = zl + far - 2 * zl * far
        piece = col_of(y - way, zl_at, core)
        c_copy(g, piece, C_FAR + far, col_of(y + way, zl, core)).start()
        c_copy(g, piece, C_CORE, col_of(y, zl, 1 - core)).start()
        piece = col_of(y + way, zl_at, core)
        c_copy(g, piece, C_CORE, col_of(y, zl, 1 - core)).start()

    def c_far(g, far):
        got_c(g, C_FAR + far)
        piece = col_of(y + 2, zl + far - 2 * zl * far, core)
        c_copy(g, piece, C_CORE, col_of(y, zl, 1 - core)).start()

    def products_c(g):
        got_c(g, C_CORE, 8)
        c_high, c_low = split(cbuf[:, g].reshape(16 * states, aux))
        c_both = jnp.concatenate([c_high, c_low], axis=0)
        both = jnp.dot(c_both, whigh[...], preferred_element_type=jnp.float32)
        t = jnp.dot(c_high, wlow[...], preferred_element_type=jnp.float32)
        t += both[: 16 * states] + both[16 * states :]
        t_high, t_low = split(t * scale_ref[g])
        thigh[g] = t_high
        tlow[g] = t_low

    def products_b(g):
        got_b(g, B_LAST, 8)
        b_high, b_low = split(bbuf[:, g].reshape(16 * states, aux))
        b_both = jnp.concatenate([b_high, b_low], axis=0)
        both = lax.dot_general(b_both, thigh[g], NT, preferred_element_type=jnp.float32)
        s = lax.dot_general(b_high, tlow[g], NT, preferred_element_type=jnp.float32)
        s += both[: 16 * states] + both[16 * states :]
        sig[...] += s

    z_own(XN)
    for g in range(XN):
        first_x_own(g)
    for g in range(XN + 1, FIRST + L["z_own"]):
        z_own(g)
    for g in range(XN, FIRST + L["x_own"]):
        x_own(g)
    for at in range(FIRST + L["c_own"]):
        c_own(at + at // CR)

    @pl.loop(FIRST, orbitals + LAST)
    def tick(t):
        def when(g, first, do):
            @pl.when((g >= first) & (g < orbitals))
            def _():
                do(g)

        def c_when(lead, do):
            at = t + lead
            first = at + at // CR

            @pl.when((at >= 0) & (first < orbitals))
            def _():
                do(first)

            @pl.when((at >= 0) & (at % CR == CR - 1) & (first + 1 < orbitals))
            def _():
                do(first + 1)

        def at_tick(ticks, do, *args):
            @pl.when(t == ticks)
            def _():
                do(*args)

        when(t + L["z_own"], XN, z_own)
        when(t + L["x_own"], XN, x_own)
        c_when(L["c_own"], c_own)

        when(t + L["z_relay"], XN, z_relay)
        when(t, XN, x_near)
        when(t + L["x_far"], XN, x_far)
        when(t + L["x_relay_own"], XN, x_relay_own)
        when(t + L["x_relay_near"], XN, x_relay_near)
        when(t + L["x_relay_far"], XN, x_relay_far)
        for g in range(XN):
            at_tick(XT[g][1], first_x_relay, g)
            for at in range(4):
                if at == 1:
                    at_tick(XT[g][2 + at], got_b, g, B_NEAR)
                if at == 3:
                    at_tick(XT[g][2 + at], got_b, g, B_FAR)
                at_tick(XT[g][2 + at], then_z, g, at, at == 0)
                at_tick(XT[g][6 + at], then_z_relay, g, at)
        @pl.when(t == W_AT)
        def _():
            for load in loads:
                load.wait()
            w_high, w_low = split(wfull[...])
            whigh[...] = w_high
            wlow[...] = w_low

        c_when(L["c_pair"], c_pair)
        c_when(L["c_near"], lambda g: c_spread(g, 0))
        c_when(L["c_near2"], lambda g: c_spread(g, 1))
        c_when(L["c_far"], lambda g: c_far(g, 0))
        c_when(L["c_far2"], lambda g: c_far(g, 1))
        c_when(L["products_c"], products_c)
        when(t + L["products_b"], XN, products_b)
        for g in range(XN):
            at_tick(XT[g][10], products_b, g)

    def copy1(step):
        to = (col + step) % 16
        return pltpu.make_async_remote_copy(
            src_ref=sig.at[pl.ds(pl.multiple_of(to * states, states), states)],
            dst_ref=part1.at[col],
            send_sem=send1,
            recv_sem=recv1,
            device_id=(row, to),
            device_id_type=MESH,
        )

    def copy2(step):
        to = (row + step) % 16
        return pltpu.make_async_remote_copy(
            src_ref=half.at[to // 8],
            dst_ref=part2.at[row],
            send_sem=send2,
            recv_sem=recv2,
            device_id=(to, col),
            device_id_type=MESH,
        )

    def wait_all(parts, semaphore):
        others = parts.at[pl.ds(0, 15)]
        pltpu.make_async_copy(others, others, semaphore).wait()

    for step in range(1, 16):
        copy1(step).start()
    part1[col] = sig[pl.ds(pl.multiple_of(col * states, states), states), :]
    wait_all(part1, recv1)
    total = jnp.sum(part1[...], axis=0)
    half[0] = total[:, :128]
    half[1] = total[:, 128:]
    for step in range(1, 16):
        copy2(step).start()
    part2[row] = half[row // 8]
    wait_all(part2, recv2)
    turned[...] = jnp.sum(part2[...], axis=0).T
    out_ref[...] = turned[pl.ds(pl.multiple_of(row % 8 * states, states), states), :]

    wait_all(part1, send1)
    wait_all(part2, send2)
    wait_all(cbuf, c_send)
    wait_all(bbuf, b_send)


def body(screened, fit_coeffs, coulomb_factors, orbital_weights):
    orbitals, aux, states = fit_coeffs.shape
    f32, bf16 = jnp.float32, jnp.bfloat16
    dma = pltpu.SemaphoreType.DMA
    return pl.pallas_call(
        kernel,
        out_shape=jax.ShapeDtypeStruct((states, states), f32),
        in_specs=[pl.BlockSpec(memory_space=pl.ANY)] * 3 + [pl.BlockSpec(memory_space=pltpu.SMEM)],
        out_specs=pl.BlockSpec(memory_space=pltpu.VMEM),
        scratch_shapes=[
            pltpu.VMEM((16, orbitals, states, aux), f32),
            pltpu.VMEM((16, orbitals, states, aux), f32),
            pltpu.VMEM((aux, aux), f32),
            pltpu.VMEM((aux, aux), bf16),
            pltpu.VMEM((aux, aux), bf16),
            pltpu.VMEM((orbitals, 16 * states, aux), bf16),
            pltpu.VMEM((orbitals, 16 * states, aux), bf16),
            pltpu.VMEM((16 * states, 16 * states), f32),
            pltpu.VMEM((16, states, 16 * states), f32),
            pltpu.VMEM((2, states, 128), f32),
            pltpu.VMEM((16, states, 128), f32),
            pltpu.VMEM((128, states), f32),
            dma((3,)),
            dma((C_KINDS, orbitals)),
            dma((B_KINDS, orbitals)),
            dma,
            dma,
            dma,
            dma,
            dma,
            dma,
        ],
        compiler_params=pltpu.CompilerParams(
            collective_id=0, has_side_effects=True, vmem_limit_bytes=63 * 1024 * 1024
        ),
        cost_estimate=pl.CostEstimate(flops=20_000_000_000, bytes_accessed=4_000_000, transcendentals=0),
    )(
        screened,
        jnp.transpose(fit_coeffs, (0, 2, 1)),
        jnp.transpose(coulomb_factors, (0, 2, 1)),
        orbital_weights,
    )


def solution(mesh):
    placed = (P("row", "col"), P(None, "row", "col"), P(None, "col", "row"), P())
    return jax.shard_map(
        body, mesh=mesh, in_specs=placed, out_specs=P("row", "col"), check_vma=False
    )
```
